1024 devices in a mesh: row: 64 (over y, x, core), col: 16 (over z).
Axes of the slice: x: 4, y: 8, z: 16, core: 2. Of those that a mesh axis runs over, the one named last changes fastest.
Arguments:
- features: bfloat16 [65536, 128], P(('row', 'col')), may hold values from -6 to 6
- degrees: int32 [65536], P('row'), may hold values from 1 to 4
- tiles: bfloat16 [1024, 16, 128, 128], P(('row', 'col')), may hold values from -0.09375 to 0.09375
- tile_slots: int32 [1024, 16], P(('row', 'col')), may hold values from 0 to 255, as said below
- tile_counts: int32 [1024], P(('row', 'col')), may hold values from 4 to 16, as said below
- w_first: bfloat16 [128, 256], replicated, may hold values from -0.5 to 0.5
- w_second: bfloat16 [256, 172], replicated, may hold values from -0.375 to 0.375
- cotangent: bfloat16 [65536, 172], P('row'), may hold values from -6 to 6
Outputs:
- logits: bfloat16 [65536, 172], P(('row', 'col'))
- grad_first: float32 [128, 256], replicated
- grad_second: float32 [256, 172], replicated
The draws below stay inside these ranges and needn't reach their ends.
Inputs may be any that keep to these rules, and one draw needn't show every extreme that they name: `tile_slots`: each row lists 16 distinct tile positions of its device's block of 8 x 32 tiles. `tile_counts`: some device uses all 16 slots.
All inputs are finite; a program needn't handle non-finite values.
Results may differ from the reference program's by a relative error of at most 0.007.
Values may be sent and summed in bfloat16 or wider, within the bound.
A program may use at most 32 MiB of HBM per device.

```python
import jax
import jax.numpy as jnp
from jax import lax

F_IN = 128
HID = 256
CLS = 172
NP = 64
NODES = 65536
TILE_ROWS = 8
TILE_COLS = 32
TILES_DEV = 16
N_ROW = 64
N_COL = 16


def draw_tile_slots(key, part):
    key = jax.random.fold_in(key, 11)
    keys = jax.random.split(key, N_ROW * N_COL)

    def choose(single):
        return jax.random.permutation(single, TILE_ROWS * TILE_COLS)[:TILES_DEV].astype(jnp.int32)
    return jax.vmap(choose)(keys)


def draw_tile_counts(key, part):
    key = jax.random.fold_in(key, 23)
    first, second = jax.random.split(key)
    counts = jax.random.randint(first, (N_ROW * N_COL,), max(1, TILES_DEV // 4), TILES_DEV + 1)
    busiest = jax.random.randint(second, (), 0, N_ROW * N_COL)
    return jnp.where(jnp.arange(N_ROW * N_COL) == busiest, TILES_DEV, counts).astype(jnp.int32)


def set_ends(values, stream_key, least, largest):
    longest = values.shape.index(max(values.shape))
    spots = []
    for shift in (0, 1):
        where = [jax.random.randint(jax.random.fold_in(stream_key, axis), (), 0, length) for axis, length in enumerate(values.shape)]
        where[longest] = (where[longest] + shift) % values.shape[longest]
        spots.append(tuple(where))
    return values.at[spots[0]].set(least).at[spots[1]].set(largest)


def levels(key, dims, cuts, low, high):
    def one(position, blocks):
        draws = jax.random.uniform(jax.random.fold_in(jax.random.fold_in(key, 6), position), (blocks,), jnp.float32, low / len(cuts), high / len(cuts))
        return jnp.repeat(jnp.exp(draws), dims[position] // blocks).reshape((-1,) + (1,) * (len(dims) - position - 1))

    loudness = one(*cuts[0])
    for cut in cuts[1:]:
        loudness = loudness * one(*cut)
    return loudness


def normal_values(key, dims, spread, reach, cuts=(), held_as=jnp.bfloat16):
    array = jax.random.normal(key, dims, jnp.float32) * spread
    if len(cuts) > 0:
        array = levels(key, dims, cuts, -0.22, 0.18) * array
    return jnp.clip(array, min=-reach, max=reach).astype(held_as)


def setup_inputs(seed: int = 0) -> dict:
    key_of = jax.random.split(jax.random.key(seed), 9)
    return {
        "features": normal_values(key_of[0], (NODES, F_IN), 1.0, 6.0, ((0, 1024),)),
        "degrees": set_ends(jax.random.randint(key_of[1], (NODES,), 1, 5), jax.random.fold_in(key_of[1], 1), 1, 4).astype(jnp.int32),
        "tiles": normal_values(key_of[2], (N_ROW * N_COL, TILES_DEV, 128, 128), (TILES_DEV * 16384 // NP) ** -0.5, 0.09375, ((0, 1024),)),
        "tile_slots": draw_tile_slots(jax.random.fold_in(key_of[8], 71), 0),
        "tile_counts": draw_tile_counts(jax.random.fold_in(key_of[8], 71), 0),
        "w_first": normal_values(key_of[5], (F_IN, HID), F_IN ** -0.5, 0.5),
        "w_second": normal_values(key_of[6], (HID, CLS), HID ** -0.5, 0.375),
        "cotangent": normal_values(key_of[7], (NODES, CLS), 1.0, 6.0, ((0, 64),)),
    }


def gelu_plain(value):
    return jax.nn.gelu(value, approximate=True)

def gelu_slope(value):
    return jax.jvp(gelu_plain, (value,), (jnp.ones_like(value),))[1]

def pick_tables(slots_one, count_one):
    live_mask = (jnp.arange(TILES_DEV) < count_one).astype(jnp.float32)
    row_of = slots_one // TILE_COLS
    col_of = slots_one % TILE_COLS
    row_pick = (jnp.arange(TILE_ROWS)[:, None] == row_of[None, :]).astype(jnp.float32) * live_mask[None, :]
    col_pick = (jnp.arange(TILE_COLS)[:, None] == col_of[None, :]).astype(jnp.float32) * live_mask[None, :]
    return (row_of, col_of, row_pick, col_pick)

def block_forward(tiles_one, slots_one, count_one, columns):
    row_of, col_of, row_pick, col_pick = pick_tables(slots_one, count_one)
    blocks = columns[col_of].astype(jnp.float32)
    prods = jnp.einsum('tij,tjf->tif', tiles_one.astype(jnp.float32), blocks, precision=lax.Precision.HIGHEST)
    summed = jnp.einsum('rt,tif->rif', row_pick, prods, precision=lax.Precision.HIGHEST)
    return summed.reshape(TILE_ROWS * 128, columns.shape[-1])

def block_backward(tiles_one, slots_one, count_one, stripe):
    row_of, col_of, row_pick, col_pick = pick_tables(slots_one, count_one)
    blocks = stripe[row_of].astype(jnp.float32)
    prods = jnp.einsum('tij,tif->tjf', tiles_one.astype(jnp.float32), blocks, precision=lax.Precision.HIGHEST)
    summed = jnp.einsum('ct,tjf->cjf', col_pick, prods, precision=lax.Precision.HIGHEST)
    return summed.reshape(TILE_COLS * 128, stripe.shape[-1])

def aggregate(source, tile_grid, slot_grid, count_grid):
    width = source.shape[-1]
    layout = source.reshape(N_ROW, N_COL, NP, width)
    columns = layout.transpose(1, 0, 2, 3).reshape(N_COL, TILE_COLS, 128, width)

    def stripe_of(index):
        parts = jax.vmap(block_forward)(tile_grid[index], slot_grid[index], count_grid[index], columns)
        return lax.optimization_barrier(jnp.sum(parts, axis=0))
    stripes = lax.map(stripe_of, jnp.arange(N_ROW, dtype=jnp.int32))
    return stripes.reshape(NODES, width)

def aggregate_back(source, tile_grid, slot_grid, count_grid):
    width = source.shape[-1]
    stripes = source.reshape(N_ROW, TILE_ROWS, 128, width)

    def column_of(index):
        parts = jax.vmap(block_backward)(tile_grid[:, index], slot_grid[:, index], count_grid[:, index], stripes)
        return lax.optimization_barrier(jnp.sum(parts, axis=0))
    cols = lax.map(column_of, jnp.arange(N_COL, dtype=jnp.int32))
    return cols.reshape(N_COL, N_ROW, NP, width).transpose(1, 0, 2, 3).reshape(NODES, width)

def reference(features, degrees, tiles, tile_slots, tile_counts, w_first, w_second, cotangent):
    tile_grid = tiles.reshape(N_ROW, N_COL, TILES_DEV, 128, 128)
    slot_grid = tile_slots.reshape(N_ROW, N_COL, TILES_DEV)
    count_grid = tile_counts.reshape(N_ROW, N_COL)
    node_scale = lax.rsqrt(degrees.astype(jnp.float32))[:, None]
    scaled_in = (node_scale * features.astype(jnp.float32)).astype(jnp.bfloat16)
    first_agg = (node_scale * aggregate(scaled_in, tile_grid, slot_grid, count_grid)).astype(jnp.bfloat16)
    first_pre = jnp.dot(first_agg, w_first, preferred_element_type=jnp.float32)
    scaled_hidden = (node_scale * gelu_plain(first_pre)).astype(jnp.bfloat16)
    second_agg = (node_scale * aggregate(scaled_hidden, tile_grid, slot_grid, count_grid)).astype(jnp.bfloat16)
    logits = jnp.dot(second_agg, w_second, preferred_element_type=jnp.float32).astype(jnp.bfloat16)
    grad_second = jnp.dot(second_agg.T, cotangent, preferred_element_type=jnp.float32)
    scaled_cot = (node_scale * cotangent.astype(jnp.float32)).astype(jnp.bfloat16)
    narrow = aggregate_back(scaled_cot, tile_grid, slot_grid, count_grid)
    grad_hidden = node_scale * jnp.dot(narrow, w_second.astype(jnp.float32).T, precision=lax.Precision.HIGHEST)
    grad_pre = (grad_hidden * gelu_slope(first_pre)).astype(jnp.bfloat16)
    grad_first = jnp.dot(first_agg.T, grad_pre, preferred_element_type=jnp.float32)
    return (logits, grad_first, grad_second)
```

```python
import functools

import jax
import jax.numpy as jnp
from jax import lax
from jax.experimental import pallas as pl
from jax.experimental.pallas import tpu as pltpu
from jax.sharding import PartitionSpec as P

MESH = pl.DeviceIdType.MESH
F32, BF16 = jnp.float32, jnp.bfloat16
CURVE = 0.7978845608028654
CUBIC = 0.044715


def dot(left, right, contract=((1,), (0,))):
    return lax.dot_general(left, right, (contract, ((), ())), preferred_element_type=F32)


def split(value):
    high = value.astype(BF16)
    return high, (value - high.astype(F32)).astype(BF16)


def kernel(
    dims, feat, deg, tiles_hbm, table, w1, w2, cot_hbm, logits, out_first, out_second,
    tiles, flipped, forward, backward, cot, scot, scale, w2p,
    g1, g2, p1, r1, p2, r2, terms, sib, tsum, tx, ty,
    grad, gsib, gx, gsum, gy, gz, gfull,
    local_sem, send_sem, g1y, g1x, g1s, g2y, g2x, g2s, one_sem,
):
    nx, ny, nz = dims
    row, z = lax.axis_index("row"), lax.axis_index("col")
    core = lax.rem(row, 2)
    chip = row // 2
    x, y = lax.rem(chip, nx), chip // nx
    other = 1 - core
    node_rows, cls = logits.shape
    width = scot.shape[1]
    stripe = nz * node_rows
    slots = tiles_hbm.shape[0]

    def device(yy, xx, kk):
        return (yy * nx + xx) * 2 + kk, z

    def send(src, dst, to, send_id, recv):
        pltpu.make_async_remote_copy(
            src_ref=src, dst_ref=dst, send_sem=send_sem.at[send_id], recv_sem=recv,
            device_id=to, device_id_type=MESH,
        ).start()

    def await_bytes(ref, sem):
        pltpu.make_async_copy(ref, ref, sem).wait()

    tiles_copy = pltpu.make_async_copy(tiles_hbm, tiles.at[pl.ds(0, slots)], local_sem.at[0])
    tiles_copy.start()
    cot_copy = pltpu.make_async_copy(cot_hbm, cot, local_sem.at[1])
    cot_copy.start()

    barrier = pltpu.get_barrier_semaphore()

    def greet(to):
        pl.semaphore_signal(barrier, inc=1, device_id=to, device_id_type=MESH)

    for step in range(1, ny):
        greet(device(lax.rem(y + step, ny), x, core))
    for step in range(1, nx):
        greet(device(y, lax.rem(x + step, nx), core))
    greet(device(y, x, other))

    @pl.loop(1, nz)
    def _(step):
        greet((row, lax.rem(z + step, nz)))

    for block in range(stripe // 128):
        line = lax.rsqrt(deg[block:block + 1, :].astype(F32))
        scale[block * 128:(block + 1) * 128, :] = jnp.broadcast_to(line, (128, 128)).T
    own = scale[pl.ds(pl.multiple_of(z * node_rows, node_rows), node_rows), :]
    own_wide = jnp.concatenate([own] * (width // 128), axis=1)
    g1[y, x, core] = (own * feat[...].astype(F32)).astype(BF16)

    pl.semaphore_wait(barrier, (ny - 1) + (nx - 1) + 1 + (nz - 1))

    y_order = sorted(range(1, ny), key=lambda step: min(step, ny - step))

    def gather_start(g, ysem, xsem, ids):
        for step in y_order:
            mine = g.at[y, x, core]
            send(mine, mine, device(lax.rem(y + step, ny), x, core), ids, ysem.at[y])
        for step in range(1, nx):
            mine = g.at[y, x, core]
            send(mine, mine, device(y, lax.rem(x + step, nx), core), ids + 1, xsem.at[x])

    def gather_rows(g, ysem, xsem, ssem, ids):
        for step in y_order:
            yy = lax.rem(y + step, ny)
            block = g.at[yy, x, core]
            await_bytes(block, ysem.at[yy])
            for side in range(1, nx):
                send(block, block, device(y, lax.rem(x + side, nx), core), ids + 1, xsem.at[x])
        column = g.at[:, x, core]
        send(column, column, device(y, x, other), ids + 2, ssem.at[x])

    def gather_columns(g, xsem, ssem, ids):
        for side in range(1, nx):
            xx = lax.rem(x + side, nx)
            column = g.at[:, xx, core]
            await_bytes(column, xsem.at[xx])
            send(column, column, device(y, x, other), ids + 2, ssem.at[xx])

    def gather_finish(g, ssem):
        for xx in range(nx):
            await_bytes(g.at[:, xx, other], ssem.at[xx])

    def gather_sent(g, ids):
        await_bytes(g.at[pl.ds(0, ny - 1), 0, 0], send_sem.at[ids])
        await_bytes(g.at[:, pl.ds(0, nx - 1), 0], send_sem.at[ids + 1])
        await_bytes(g.at[:, :, 0], send_sem.at[ids + 2])

    def aggregate(g, p, r, ids, sem):
        total = ny * nx * 2 * node_rows
        span = min(256, stripe)
        peers = span // node_rows

        @pl.loop(0, stripe // span)
        def _(part):
            rows = forward[pl.ds(pl.multiple_of(part * span, span), span), :]
            value = dot(rows, g[...].reshape(total, g.shape[-1])).astype(BF16)
            p[pl.ds(part * peers, peers)] = value.reshape(peers, node_rows, g.shape[-1])
            for peer in range(peers):
                to = part * peers + peer

                @pl.when(to != z)
                def _():
                    send(p.at[to], r.at[z], (row, to), ids, sem)

        r[z] = p[z]

    def aggregate_sum(r, sem):
        await_bytes(r.at[pl.ds(0, nz - 1)], sem)
        return functools.reduce(lambda a, b: a + b, [r[i].astype(F32) for i in range(nz)])

    gather_start(g1, g1y, g1x, 0)

    tiles_copy.wait()
    tiles[slots] = jnp.zeros((128, 128), BF16)
    tile_rows, tile_cols = stripe // 128, ny * nx

    @pl.loop(0, tile_cols)
    def _(c):
        for r in range(tile_rows):
            forward[r * 128:(r + 1) * 128, pl.ds(pl.multiple_of(c * 128, 128), 128)] = tiles[
                table[r * tile_cols + c]
            ]

    gather_rows(g1, g1y, g1x, g1s, 0)

    @pl.loop(0, slots + 1)
    def _(t):
        flipped[t] = tiles[t].astype(F32).T.astype(BF16)

    @pl.loop(0, tile_cols)
    def _(c):
        for r in range(tile_rows):
            backward[pl.ds(pl.multiple_of(c * 128, 128), 128), r * 128:(r + 1) * 128] = flipped[
                table[r * tile_cols + c]
            ]

    cot_copy.wait()
    scot[:, 128:] = jnp.zeros((stripe, width - 128), BF16)

    @pl.loop(0, tile_rows)
    def _(r):
        rows = pl.ds(pl.multiple_of(r * 128, 128), 128)
        value, by = cot[rows, :].astype(F32), scale[rows, :]
        scot[rows, :128] = (value[:, :128] * by).astype(BF16)
        scot[rows, 128:cls] = (value[:, 128:] * by[:, :cls - 128]).astype(BF16)

    w2p[:, 128:] = jnp.zeros((w2p.shape[0], width - 128), BF16)
    w2p[:, :cls] = w2[...]

    @pl.loop(0, ny)
    def _(line):
        rows = backward[pl.ds(pl.multiple_of(line * nx * 128, nx * 128), nx * 128), :]
        value = dot(rows, scot[...]).astype(BF16)
        terms[line] = value.reshape(nx, 2, node_rows, width)
        send(terms.at[line, :, other], sib.at[line], device(y, x, other), 6, one_sem.at[0])

    gather_columns(g1, g1x, g1s, 0)
    gather_finish(g1, g1s)
    aggregate(g1, p1, r1, 7, one_sem.at[1])

    await_bytes(sib, one_sem.at[0])

    @pl.loop(0, ny)
    def _(line):
        for xx in range(nx):
            tsum[xx, line] = (
                terms[line, xx, core].astype(F32) + sib[line, xx].astype(F32)
            ).astype(BF16)

    for side in range(1, nx):
        xx = lax.rem(x + side, nx)
        send(tsum.at[xx], tx.at[x], device(y, xx, core), 8, one_sem.at[2])
    tx[x] = tsum[x]

    first_agg = (own * aggregate_sum(r1, one_sem.at[1])).astype(BF16)
    first_pre = dot(first_agg, w1[...])
    bend = jnp.tanh(CURVE * (first_pre + CUBIC * first_pre * first_pre * first_pre))
    hidden = (own_wide * (0.5 * first_pre * (1.0 + bend))).astype(BF16)
    slope = 0.5 * (1.0 + bend) + 0.5 * first_pre * (1.0 - bend * bend) * (
        CURVE * (1.0 + 3.0 * CUBIC * first_pre * first_pre)
    )
    g2[y, x, core] = dot(hidden, w2p[...]).astype(BF16)
    gather_start(g2, g2y, g2x, 3)

    await_bytes(tx.at[pl.ds(0, nx - 1)], one_sem.at[2])

    @pl.loop(0, ny)
    def _(line):
        value = functools.reduce(lambda a, b: a + b, [tx[i, line].astype(F32) for i in range(nx)])
        tsum[x, line] = value.astype(BF16)

    for step in range(1, ny):
        yy = lax.rem(y + step, ny)
        send(tsum.at[x, yy], ty.at[y], device(yy, x, core), 9, one_sem.at[3])
    ty[y] = tsum[x, y]

    gather_rows(g2, g2y, g2x, g2s, 3)

    await_bytes(ty.at[pl.ds(0, ny - 1)], one_sem.at[3])
    narrow = functools.reduce(lambda a, b: a + b, [ty[i].astype(F32) for i in range(ny)])
    high, low = split(narrow)
    back = dot(high, w2p[...], ((1,), (1,))) + dot(low, w2p[...], ((1,), (1,)))
    grad_pre = (own_wide * back * slope).astype(BF16)
    first_rows = dot(first_agg, grad_pre, ((0,), (0,)))
    second_rows = dot(hidden, high, ((0,), (0,))) + dot(hidden, low, ((0,), (0,)))
    n_first, n_second = first_rows.shape[0], second_rows.shape[0]
    chunk = grad.shape[3]
    spare = 2 * nx * ny * chunk - n_first - n_second
    grad[...] = jnp.concatenate(
        [first_rows, second_rows, jnp.zeros((spare, width), F32)], axis=0
    ).reshape(grad.shape)
    send(grad.at[other], gsib, device(y, x, other), 10, one_sem.at[4])

    gather_columns(g2, g2x, g2s, 3)

    await_bytes(gsib, one_sem.at[4])
    gsib[...] = gsib[...] + grad[core]
    for side in range(1, nx):
        xx = lax.rem(x + side, nx)
        send(gsib.at[xx], gx.at[x], device(y, xx, core), 11, one_sem.at[5])
    gx[x] = gsib[x]

    gather_finish(g2, g2s)
    aggregate(g2, p2, r2, 12, one_sem.at[6])

    await_bytes(gx.at[pl.ds(0, nx - 1)], one_sem.at[5])
    gsum[...] = functools.reduce(lambda a, b: a + b, [gx[i] for i in range(nx)])
    for step in range(1, ny):
        yy = lax.rem(y + step, ny)
        send(gsum.at[yy], gy.at[y], device(yy, x, core), 13, one_sem.at[7])
    gy[y] = gsum[y]
    await_bytes(gy.at[pl.ds(0, ny - 1)], one_sem.at[7])
    gz[z] = functools.reduce(lambda a, b: a + b, [gy[i] for i in range(ny)])

    @pl.loop(1, nz)
    def _(step):
        send(gz.at[z], gz.at[z], (row, lax.rem(z + step, nz)), 14, one_sem.at[8])

    await_bytes(gz.at[pl.ds(0, nz - 1)], one_sem.at[8])
    gfull[core, x, y] = functools.reduce(lambda a, b: a + b, [gz[i] for i in range(nz)])
    mine = gfull.at[core, x, y]
    for step in range(1, ny):
        send(mine, mine, device(lax.rem(y + step, ny), x, core), 15, one_sem.at[9])
    await_bytes(gx.at[0, pl.ds(0, ny - 1)], one_sem.at[9])
    mine_x = gfull.at[core, x]
    for side in range(1, nx):
        send(mine_x, mine_x, device(y, lax.rem(x + side, nx), core), 16, one_sem.at[10])
    await_bytes(gx.at[pl.ds(0, nx - 1)], one_sem.at[10])
    send(gfull.at[core], gfull.at[core], device(y, x, other), 17, one_sem.at[11])

    second = own_wide * aggregate_sum(r2, one_sem.at[6])
    logits[...] = second[:, :cls].astype(BF16)

    await_bytes(gsib, one_sem.at[11])
    whole = gfull[...].reshape(2 * nx * ny * chunk, width)
    out_first[...] = whole[:n_first]
    out_second[...] = whole[n_first:n_first + n_second, :cls]

    gather_sent(g1, 0)
    gather_sent(g2, 3)
    await_bytes(sib, send_sem.at[6])
    await_bytes(r1.at[pl.ds(0, nz - 1)], send_sem.at[7])
    await_bytes(tx.at[pl.ds(0, nx - 1)], send_sem.at[8])
    await_bytes(ty.at[pl.ds(0, ny - 1)], send_sem.at[9])
    await_bytes(gsib, send_sem.at[10])
    await_bytes(gx.at[pl.ds(0, nx - 1)], send_sem.at[11])
    await_bytes(r2.at[pl.ds(0, nz - 1)], send_sem.at[12])
    await_bytes(gy.at[pl.ds(0, ny - 1)], send_sem.at[13])
    await_bytes(gz.at[pl.ds(0, nz - 1)], send_sem.at[14])
    await_bytes(gx.at[0, pl.ds(0, ny - 1)], send_sem.at[15])
    await_bytes(gx.at[pl.ds(0, nx - 1)], send_sem.at[16])
    await_bytes(gsib, send_sem.at[17])


def shards(dims, features, degrees, tiles, tile_slots, tile_counts, w_first, w_second, cotangent):
    nx, ny, nz = dims
    node_rows, f_in = features.shape
    slots = tiles.shape[1]
    hid, cls = w_second.shape
    stripe = nz * node_rows
    tile_rows, tile_cols = stripe // 128, ny * nx
    width = 256
    chunk = 512 // (2 * nx * ny)
    cells = jnp.arange(tile_rows * tile_cols, dtype=jnp.int32)
    order = jnp.arange(slots, dtype=jnp.int32)
    hit = (tile_slots[0][None, :] == cells[:, None]) & (order < tile_counts[0])[None, :]
    table = jnp.sum(jnp.where(hit, order - slots, 0), axis=1, dtype=jnp.int32) + slots
    vmem = pl.BlockSpec(memory_space=pltpu.VMEM)
    far = pl.BlockSpec(memory_space=pl.ANY)
    scratch = lambda *shape, dtype=BF16: pltpu.VMEM(shape, dtype)
    sems = lambda n: pltpu.SemaphoreType.DMA((n,))
    return pl.pallas_call(
        functools.partial(kernel, dims),
        out_shape=(
            jax.ShapeDtypeStruct((node_rows, cls), BF16),
            jax.ShapeDtypeStruct((f_in, hid), F32),
            jax.ShapeDtypeStruct((hid, cls), F32),
        ),
        in_specs=[vmem, vmem, far, pl.BlockSpec(memory_space=pltpu.SMEM), vmem, vmem, far],
        out_specs=(vmem, vmem, vmem),
        scratch_shapes=[
            scratch(slots + 1, 128, 128),
            scratch(slots + 1, 128, 128),
            scratch(stripe, tile_cols * 128),
            scratch(tile_cols * 128, stripe),
            scratch(stripe, cls),
            scratch(stripe, width),
            scratch(stripe, 128, dtype=F32),
            scratch(hid, width),
            scratch(ny, nx, 2, node_rows, f_in),
            scratch(ny, nx, 2, node_rows, width),
            scratch(nz, node_rows, f_in),
            scratch(nz, node_rows, f_in),
            scratch(nz, node_rows, width),
            scratch(nz, node_rows, width),
            scratch(ny, nx, 2, node_rows, width),
            scratch(ny, nx, node_rows, width),
            scratch(nx, ny, node_rows, width),
            scratch(nx, ny, node_rows, width),
            scratch(ny, node_rows, width),
            scratch(2, nx, ny, chunk, width, dtype=F32),
            scratch(nx, ny, chunk, width, dtype=F32),
            scratch(nx, ny, chunk, width, dtype=F32),
            scratch(ny, chunk, width, dtype=F32),
            scratch(ny, chunk, width, dtype=F32),
            scratch(nz, chunk, width, dtype=F32),
            scratch(2, nx, ny, chunk, width, dtype=F32),
            sems(2),
            sems(18),
            sems(ny), sems(nx), sems(nx),
            sems(ny), sems(nx), sems(nx),
            sems(12),
        ],
        compiler_params=pltpu.CompilerParams(
            collective_id=0, has_side_effects=True, vmem_limit_bytes=48 * 1024 * 1024
        ),
    )(
        features, degrees.reshape(tile_rows, 128), tiles[0], table, w_first, w_second, cotangent
    )


def solution(mesh):
    ny = 8 if mesh.shape["row"] == 64 else 2
    dims = (mesh.shape["row"] // (2 * ny), ny, mesh.shape["col"])
    placed = (
        P(("row", "col"), None),
        P("row"),
        P(("row", "col"), None, None, None),
        P(("row", "col"), None),
        P(("row", "col")),
        P(),
        P(),
        P("row", None),
    )
    return jax.shard_map(
        functools.partial(shards, dims),
        mesh=mesh,
        in_specs=placed,
        out_specs=(P(("row", "col"), None), P(), P()),
        check_vma=False,
    )
```

```python
import functools

import jax
import jax.numpy as jnp
from jax import lax
from jax.experimental import pallas as pl
from jax.experimental.pallas import tpu as pltpu
from jax.sharding import PartitionSpec as P

MESH = pl.DeviceIdType.MESH
F32, BF16 = jnp.float32, jnp.bfloat16
CURVE = 0.7978845608028654
CUBIC = 0.044715
HALF = 96


def dot(left, right, contract=((1,), (0,))):
    return lax.dot_general(left, right, (contract, ((), ())), preferred_element_type=F32)


def split(value):
    high = value.astype(BF16)
    return high, (value - high.astype(F32)).astype(BF16)


def total(parts):
    parts = list(parts)
    while len(parts) > 1:
        parts = [a + b for a, b in zip(parts[::2], parts[1::2])] + parts[len(parts) & ~1:]
    return parts[0]


def kernel(
    dims, feat, deg, tiles_hbm, table, w1, w2t, cot_hbm, logits, out_first, out_second,
    tiles, adjacency, cot, scot, w2p, turned, own_scale,
    g1, g2, source, p1, r1, q1, p2, r2, q2, terms, sib, tsum, tx, ty, narrow_t, back_all,
    grad, gsib, gys, gy, gxs, gx, gz, gfull,
    local_sem, send_sem, g1y, g1x, g1s, g2y, g2x, g2s, one_sem,
):
    nx, ny, nz = dims
    row, z = lax.axis_index("row"), lax.axis_index("col")
    core = lax.rem(row, 2)
    chip = row // 2
    x, y = lax.rem(chip, nx), chip // nx
    other = 1 - core
    node_rows, cls = logits.shape
    stripe = nz * node_rows
    slots = tiles_hbm.shape[0]
    tile_rows, tile_cols = stripe // 128, ny * nx
    finish = []

    def device(yy, xx, kk):
        return (yy * nx + xx) * 2 + kk, z

    def send(src, dst, to, send_id, recv):
        pltpu.make_async_remote_copy(
            src_ref=src, dst_ref=dst, send_sem=send_sem.at[send_id], recv_sem=recv,
            device_id=to, device_id_type=MESH,
        ).start()

    def await_bytes(ref, sem):
        if 0 in ref.shape:
            return
        pltpu.make_async_copy(ref, ref, sem).wait()

    def sent(ref, send_id, some=1):
        if some:
            finish.append(lambda: await_bytes(ref, send_sem.at[send_id]))

    tiles_copy = pltpu.make_async_copy(tiles_hbm, tiles.at[pl.ds(0, slots)], local_sem.at[0])
    tiles_copy.start()
    cot_copy = pltpu.make_async_copy(cot_hbm, cot, local_sem.at[1])
    cot_copy.start()

    barrier = pltpu.get_barrier_semaphore()

    def greet(to):
        pl.semaphore_signal(barrier, inc=1, device_id=to, device_id_type=MESH)

    for step in range(1, ny):
        greet(device(lax.rem(y + step, ny), x, core))
    for step in range(1, nx):
        greet(device(y, lax.rem(x + step, nx), core))
    greet(device(y, x, other))

    @pl.loop(1, nz)
    def _(step):
        greet((row, lax.rem(z + step, nz)))

    per_line = 128 // node_rows
    line = lax.rsqrt(deg[pl.ds(z // per_line, 1), :].astype(F32))
    own_scale[...] = jnp.broadcast_to(line, (128, 128)).T
    own = own_scale[pl.ds(pl.multiple_of(lax.rem(z, per_line) * node_rows, node_rows), node_rows), :]
    own_wide = jnp.concatenate([own, own], axis=1)
    g1[y, x, core] = (own * feat[...].astype(F32)).astype(BF16)

    pl.semaphore_wait(barrier, (ny - 1) + (nx - 1) + 1 + (nz - 1))

    y_order = sorted(range(1, ny), key=lambda step: min(step, ny - step))

    pairs = ny // 2

    def gather_start(g, ysem, xsem, ids):
        mine = g.at[y, x, core]
        for step in y_order:
            send(mine, mine, device(lax.rem(y + step, ny), x, core), ids, ysem.at[y])
        for step in range(1, nx):
            to = device(y, lax.rem(x + step, nx), core)
            send(mine, mine, to, ids + 1, xsem.at[x, y // 2])
        sent(g.at[pl.ds(0, ny - 1), 0, 0], ids)
        sent(g.at[:, pl.ds(0, nx - 1), 0], ids + 1, nx - 1)
        sent(g.at[:, :, 0], ids + 2)

    def gather_rows(g, ysem, xsem, ssem, ids):
        for step in y_order:
            yy = lax.rem(y + step, ny)
            block = g.at[yy, x, core]
            await_bytes(block, ysem.at[yy])
            for side in range(1, nx):
                to = device(y, lax.rem(x + side, nx), core)
                send(block, block, to, ids + 1, xsem.at[x, yy // 2])
        column = g.at[:, x, core]
        send(column, column, device(y, x, other), ids + 2, ssem.at[x])

    def gather_columns(g, xsem, ssem, ids, steps):
        for step in steps:
            pair = lax.rem(y // 2 + step, pairs)
            for side in range(1, nx):
                xx = lax.rem(x + side, nx)
                blocks = g.at[pl.ds(pair * 2, 2), xx, core]
                await_bytes(blocks, xsem.at[xx, pair])
                send(blocks, blocks, device(y, x, other), ids + 2, ssem.at[xx])

    pair_order = sorted(range(pairs), key=lambda step: min(step, pairs - step))

    def gather_finish(g, ssem):
        for xx in range(nx):
            await_bytes(g.at[:, xx, other], ssem.at[xx])

    reach = nz // 4

    def aggregate(source_of, pack, p, r, ids, sem, far_sem):
        span = min(256, stripe)
        peers, parts = span // node_rows, stripe // span
        half = p.shape[1] // 2

        @pl.loop(0, parts)
        def _(i):
            part = i
            if parts == 4:
                turn = (1 - i // 2) * (2 + i) + (i // 2) * (3 - i)
                part = lax.rem(z // peers + turn, parts)
            rows = adjacency[pl.ds(pl.multiple_of(part * span, span), span), :]
            value = dot(rows, source_of())
            for peer in range(peers):
                to = part * peers + peer
                p[to] = pack(value[peer * node_rows:(peer + 1) * node_rows])
                ahead = lax.rem(to - z + nz, nz)

                if reach > 1:
                    @pl.when(lax.rem(ahead, reach) != 0)
                    def _():
                        side = 1 - ahead // (nz // 2)
                        away = side * ahead + (1 - side) * (nz - ahead)
                        far = (away - 1) // reach
                        hop = away - reach * far
                        slot = far * (2 * reach + side * (reach - 1)) + (1 - far) * side * reach + hop - 1
                        target = lax.rem(z + (2 * side - 1) * hop + nz, nz)
                        send(p.at[to], r.at[slot], (row, target), ids, one_sem.at[sem + far * (far_sem - sem)])

                @pl.when(ahead == nz // 2)
                def _():
                    for side in range(2):
                        rows = pl.ds(side * half, half)
                        target = lax.rem(z + (2 * side - 1) * reach + nz, nz)
                        send(p.at[to, rows], r.at[4 * reach - 2, rows], (row, target), ids, one_sem.at[far_sem])

        r[4 * reach - 1] = p[z]
        sent(r.at[pl.ds(0, nz - 1)], ids)

    def relay(p, r, q, ids, sem, far_sem):
        half = p.shape[1] // 2
        await_bytes(r.at[pl.ds(2 * reach, 2 * reach - 1)], one_sem.at[far_sem])
        opposite = r[4 * reach - 2].astype(F32)
        nothing = jnp.zeros((half, 128), F32)
        for side in range(2):
            to = lax.rem(z + (2 * side - 1) * reach + nz, nz)
            first = 2 * reach + side * (reach - 1)
            part = (
                jnp.concatenate([nothing, opposite[half:]], axis=0) if side
                else jnp.concatenate([opposite[:half], nothing], axis=0)
            )
            value = total([part, p[to].astype(F32)] + [r[first + i].astype(F32) for i in range(reach - 1)])
            q[side] = value.astype(BF16)
            send(q.at[side], r.at[side * reach + reach - 1], (row, to), ids, one_sem.at[sem])

    def aggregate_sum(r, sem):
        await_bytes(r.at[pl.ds(0, 2 * reach)], one_sem.at[sem])
        return total(r[i].astype(F32) for i in list(range(2 * reach)) + [4 * reach - 1])

    short = node_rows // 2
    low_lanes = lax.broadcasted_iota(jnp.int32, (short, 128), 1) < 64

    def pack_classes(value):
        first, second = value[:short, 128:], pltpu.roll(value[short:, 128:], 64, 1)
        tail = jnp.where(low_lanes, first, second)
        return jnp.concatenate([value[:, :128], tail], axis=0).astype(BF16)

    def finish_all():
        for wait in finish:
            wait()


    gather_start(g1, g1y, g1x, 0)

    tiles_copy.wait()
    tiles[slots] = jnp.zeros((128, 128), BF16)

    @pl.loop(0, tile_cols)
    def _(c):
        for r in range(tile_rows):
            adjacency[r * 128:(r + 1) * 128, pl.ds(pl.multiple_of(c * 128, 128), 128)] = tiles[
                table[r * tile_cols + c]
            ]

    gather_rows(g1, g1y, g1x, g1s, 0)

    cot_copy.wait()
    scot[cls // 16 * 16:, :] = jnp.zeros((2 * HALF - cls // 16 * 16, stripe), BF16)
    for r in range(tile_rows):
        by = lax.rsqrt(deg[r:r + 1, :].astype(F32))
        scot[:cls, r * 128:(r + 1) * 128] = (
            cot[:, r * 128:(r + 1) * 128].astype(F32) * by
        ).astype(BF16)
    w2p[cls // 16 * 16:, :] = jnp.zeros((w2p.shape[0] - cls // 16 * 16, w2p.shape[1]), BF16)
    w2p[:cls, :] = w2t[...]

    @pl.loop(0, ny)
    def _(part):
        columns = pl.ds(pl.multiple_of(part * nx * 128, nx * 128), nx * 128)
        value = dot(scot[...], adjacency[:, columns]).astype(BF16)
        for xx in range(nx):
            terms[part, xx] = value[:, xx * 128:(xx + 1) * 128].reshape(2, HALF, 128)
        send(terms.at[part, :, other], sib.at[part], device(y, x, other), 6, one_sem.at[0])

    sent(sib, 6)

    gather_columns(g1, g1x, g1s, 0, pair_order)

    await_bytes(sib, one_sem.at[0])

    @pl.loop(0, ny)
    def _(part):
        for xx in range(nx):
            tsum[xx, part] = (
                terms[part, xx, core].astype(F32) + sib[part, xx].astype(F32)
            ).astype(BF16)

    for side in range(1, nx):
        xx = lax.rem(x + side, nx)
        send(tsum.at[xx], tx.at[x], device(y, xx, core), 8, one_sem.at[2])
    sent(tx.at[pl.ds(0, nx - 1)], 8, nx - 1)
    tx[x] = tsum[x]

    gather_finish(g1, g1s)
    nodes = tile_cols * 128
    aggregate(lambda: g1[...].reshape(nodes, 128), lambda v: v.astype(BF16), p1, r1, 7, 1, 13)
    relay(p1, r1, q1, 7, 1, 13)

    await_bytes(tx.at[pl.ds(0, nx - 1)], one_sem.at[2])

    @pl.loop(0, ny)
    def _(part):
        tsum[x, part] = total(tx[i, part].astype(F32) for i in range(nx)).astype(BF16)

    for step in y_order:
        yy = lax.rem(y + step, ny)
        send(tsum.at[x, yy], ty.at[y], device(yy, x, core), 9, one_sem.at[3])
    sent(ty.at[pl.ds(0, ny - 1)], 9)
    ty[y] = tsum[x, y]

    first_agg = (own * aggregate_sum(r1, 1)).astype(BF16)
    first_pre = dot(first_agg, w1[...])
    bend = jnp.tanh(CURVE * (first_pre + CUBIC * first_pre * first_pre * first_pre))
    hidden = (own_wide * (0.5 * first_pre * (1.0 + bend))).astype(BF16)
    g2[y, x, core] = pack_classes(dot(hidden, w2p[...], ((1,), (1,))))
    gather_start(g2, g2y, g2x, 3)

    slope = 0.5 * (1.0 + bend) + 0.5 * first_pre * (1.0 - bend * bend) * (
        CURVE * (1.0 + 3.0 * CUBIC * first_pre * first_pre)
    )

    await_bytes(ty.at[pl.ds(0, ny - 1)], one_sem.at[3])
    narrow_t[core] = total(ty[i].astype(F32) for i in range(ny))
    mine = narrow_t.at[core]
    send(mine, mine, device(y, x, other), 18, one_sem.at[12])
    sent(mine, 18)

    gather_rows(g2, g2y, g2x, g2s, 3)

    n_first, hid = out_first.shape
    await_bytes(narrow_t.at[0], one_sem.at[12])
    lane_core = lax.broadcasted_iota(jnp.int32, (2 * HALF, 128), 1) // node_rows
    narrow = jnp.where(lane_core == core, narrow_t[...].reshape(2 * HALF, 128), 0.0)
    high, low = split(narrow)
    w2_rows = w2p[:2 * HALF, :]
    back_all[...] = dot(high, w2_rows, ((0,), (0,))) + dot(low, w2_rows, ((0,), (0,)))
    back = back_all[pl.ds(pl.multiple_of(core * node_rows, node_rows), node_rows), :]
    grad_pre = (own_wide * back * slope).astype(BF16)
    first_rows = dot(first_agg, grad_pre, ((0,), (0,)))
    hidden_twice = jnp.concatenate([hidden, hidden], axis=0)
    second_rows = dot(high, hidden_twice) + dot(low, hidden_twice)
    chunk = gz.shape[1] // 2
    spare = 2 * nx * ny * chunk - n_first - 2 * HALF
    grad[...] = jnp.concatenate(
        [first_rows, second_rows, jnp.zeros((spare, hid), F32)], axis=0
    ).reshape(grad.shape)
    send(grad.at[other], gsib, device(y, x, other), 10, one_sem.at[4])
    sent(gsib, 10)

    gather_columns(g2, g2x, g2s, 3, pair_order[:1])

    await_bytes(gsib, one_sem.at[4])
    gys[...] = (gsib[...] + grad[core]).astype(BF16)
    for step in y_order:
        yy = lax.rem(y + step, ny)
        send(gys.at[yy], gy.at[y], device(yy, x, core), 11, one_sem.at[5])
    sent(gy.at[pl.ds(0, ny - 1)], 11)
    gy[y] = gys[y]

    gather_columns(g2, g2x, g2s, 3, pair_order[1:])

    await_bytes(gy.at[pl.ds(0, ny - 1)], one_sem.at[5])
    gxs[...] = total(gy[i].astype(F32) for i in range(ny)).reshape(nx, chunk, hid)
    for side in range(1, nx):
        xx = lax.rem(x + side, nx)
        send(gxs.at[xx], gx.at[x], device(y, xx, core), 13, one_sem.at[7])
    sent(gx.at[pl.ds(0, nx - 1)], 13, nx - 1)
    gx[x] = gxs[x]

    gather_finish(g2, g2s)

    @pl.loop(0, tile_cols)
    def _(i):
        for k in range(2):
            block = g2[i // nx, lax.rem(i, nx), k]
            tail = block[node_rows:].astype(F32)
            tail = jnp.concatenate([tail, pltpu.roll(tail, 64, 1)], axis=0).astype(BF16)
            rows = pl.ds(pl.multiple_of(i * 128 + k * node_rows, node_rows), node_rows)
            source[rows, :128] = block[:node_rows]
            source[rows, 128:] = tail

    await_bytes(gx.at[pl.ds(0, nx - 1)], one_sem.at[7])
    summed = total(gx[i] for i in range(nx))
    gz[z] = jnp.concatenate([summed[:, :128], summed[:, 128:]], axis=0).astype(BF16)

    @pl.loop(1, nz)
    def _(step):
        send(gz.at[z], gz.at[z], (row, lax.rem(z + step, nz)), 14, one_sem.at[8])

    sent(gz.at[pl.ds(0, nz - 1)], 14)

    aggregate(lambda: source[...], pack_classes, p2, r2, 12, 6, 14)
    relay(p2, r2, q2, 12, 6, 14)

    await_bytes(gz.at[pl.ds(0, nz - 1)], one_sem.at[8])
    summed = total(gz[i].astype(F32) for i in range(nz))
    gfull[core, y, x] = jnp.concatenate([summed[:chunk], summed[chunk:]], axis=1)
    mine_y = gfull.at[core, y, x]
    for step in y_order:
        send(mine_y, mine_y, device(lax.rem(y + step, ny), x, core), 15, one_sem.at[9])
    sent(gfull.at[0, pl.ds(0, ny - 1), 0], 15)
    await_bytes(gfull.at[0, pl.ds(0, ny - 1), 0], one_sem.at[9])
    mine_x = gfull.at[core, :, x]
    for side in range(1, nx):
        send(mine_x, mine_x, device(y, lax.rem(x + side, nx), core), 16, one_sem.at[10])
    sent(gfull.at[0, :, pl.ds(0, nx - 1)], 16, nx - 1)
    await_bytes(gfull.at[0, :, pl.ds(0, nx - 1)], one_sem.at[10])
    send(gfull.at[core], gfull.at[core], device(y, x, other), 17, one_sem.at[11])
    sent(gfull.at[0], 17)
    await_bytes(gfull.at[0], one_sem.at[11])
    whole = gfull[...].reshape(2 * nx * ny * chunk, hid)
    out_first[...] = whole[:n_first]
    out_second[...] = whole[n_first:n_first + cls]

    packed = aggregate_sum(r2, 6)
    tail = packed[node_rows:]
    tail = jnp.concatenate([tail, pltpu.roll(tail, 64, 1)], axis=0)
    logits[:, :128] = (own * packed[:node_rows]).astype(BF16)
    logits[:, 128:] = (own * tail)[:, :cls - 128].astype(BF16)

    finish_all()


def shards(dims, features, degrees, tiles, tile_slots, tile_counts, w_first, w_second, cotangent):
    nx, ny, nz = dims
    node_rows, f_in = features.shape
    slots = tiles.shape[1]
    hid, cls = w_second.shape
    stripe = nz * node_rows
    tile_rows, tile_cols = stripe // 128, ny * nx
    chunk = 512 // (2 * nx * ny)
    cells = jnp.arange(tile_rows * tile_cols, dtype=jnp.int32)
    order = jnp.arange(slots, dtype=jnp.int32)
    hit = (tile_slots[0][None, :] == cells[:, None]) & (order < tile_counts[0])[None, :]
    table = jnp.sum(jnp.where(hit, order - slots, 0), axis=1, dtype=jnp.int32) + slots
    vmem = pl.BlockSpec(memory_space=pltpu.VMEM)
    far = pl.BlockSpec(memory_space=pl.ANY)
    scratch = lambda *shape, dtype=BF16: pltpu.VMEM(shape, dtype)
    sems = lambda *shape: pltpu.SemaphoreType.DMA(shape)
    logits, grad_first, grad_second = pl.pallas_call(
        functools.partial(kernel, dims),
        out_shape=(
            jax.ShapeDtypeStruct((node_rows, cls), BF16),
            jax.ShapeDtypeStruct((f_in, hid), F32),
            jax.ShapeDtypeStruct((cls, hid), F32),
        ),
        in_specs=[vmem, vmem, far, pl.BlockSpec(memory_space=pltpu.SMEM), vmem, vmem, far],
        out_specs=(vmem, vmem, vmem),
        scratch_shapes=[
            scratch(slots + 1, 128, 128),
            scratch(stripe, tile_cols * 128),
            scratch(cls, stripe),
            scratch(2 * HALF, stripe),
            scratch(256, hid),
            scratch(8, 128, dtype=F32),
            scratch(128, 128, dtype=F32),
            scratch(ny, nx, 2, node_rows, f_in),
            scratch(ny, nx, 2, HALF, 128),
            scratch(tile_cols * 128, 256),
            scratch(nz, node_rows, f_in),
            scratch(nz, node_rows, f_in),
            scratch(2, node_rows, f_in),
            scratch(nz, HALF, 128),
            scratch(nz, HALF, 128),
            scratch(2, HALF, 128),
            scratch(ny, nx, 2, HALF, 128),
            scratch(ny, nx, HALF, 128),
            scratch(nx, ny, HALF, 128),
            scratch(nx, ny, HALF, 128),
            scratch(ny, HALF, 128),
            scratch(2, HALF, 128, dtype=F32),
            scratch(128, hid, dtype=F32),
            scratch(2, ny, nx * chunk, hid, dtype=F32),
            scratch(ny, nx * chunk, hid, dtype=F32),
            scratch(ny, nx * chunk, hid),
            scratch(ny, nx * chunk, hid),
            scratch(nx, chunk, hid, dtype=F32),
            scratch(nx, chunk, hid, dtype=F32),
            scratch(nz, 2 * chunk, hid // 2),
            scratch(2, ny, nx, chunk, hid, dtype=F32),
            sems(2),
            sems(19),
            sems(ny), sems(nx, ny // 2), sems(nx),
            sems(ny), sems(nx, ny // 2), sems(nx),
            sems(15),
        ],
        compiler_params=pltpu.CompilerParams(
            collective_id=0, has_side_effects=True, vmem_limit_bytes=48 * 1024 * 1024
        ),
    )(
        features, degrees.reshape(tile_rows, 128), tiles[0], table, w_first, w_second.T, cotangent.T
    )
    return logits, grad_first, grad_second.T


def solution(mesh):
    ny = 8 if mesh.shape["row"] == 64 else 2
    dims = (mesh.shape["row"] // (2 * ny), ny, mesh.shape["col"])
    placed = (
        P(("row", "col"), None),
        P("row"),
        P(("row", "col"), None, None, None),
        P(("row", "col"), None),
        P(("row", "col")),
        P(),
        P(),
        P("row", None),
    )
    return jax.shard_map(
        functools.partial(shards, dims),
        mesh=mesh,
        in_specs=placed,
        out_specs=(P(("row", "col"), None), P(), P()),
        check_vma=False,
    )
```

```python
import functools

import jax
import jax.numpy as jnp
from jax import lax
from jax.experimental import pallas as pl
from jax.experimental.pallas import tpu as pltpu
from jax.sharding import PartitionSpec as P

MESH = pl.DeviceIdType.MESH
F32, BF16 = jnp.float32, jnp.bfloat16
CURVE = 0.7978845608028654
CUBIC = 0.044715
LIMIT = 63 * 1024 * 1024
HALF = 96


def dot(left, right, contract=((1,), (0,))):
    return lax.dot_general(left, right, (contract, ((), ())), preferred_element_type=F32)


def split(value):
    high = value.astype(BF16)
    return high, (value - high.astype(F32)).astype(BF16)


def total(parts):
    parts = list(parts)
    while len(parts) > 1:
        parts = [a + b for a, b in zip(parts[::2], parts[1::2])] + parts[len(parts) & ~1:]
    return parts[0]


def kernel(
    dims, feat_hbm, deg_hbm, tiles_hbm, slots_hbm, counts_hbm, w1_hbm, w2t_hbm, cot_hbm,
    logits, out_first, out_second,
    feat, deg, tiles, slots_at, count_at, w1, w2t, cot, table_v, table,
    adjacency, scot, w2p, own_scale,
    g1, g2, source, p1, r1, q1, p2, r2, q2, terms, sib, tsum, tx, ty, narrow_t, back_all,
    grad, gsib, gys, gy, gxs, gx, gz, gw, gfull,
    local_sem, send_sem, g1y, g1x, g1s, g2y, g2x, g2s, one_sem,
):
    nx, ny, nz = dims
    row, z = lax.axis_index("row"), lax.axis_index("col")
    core = lax.rem(row, 2)
    chip = row // 2
    x, y = lax.rem(chip, nx), chip // nx
    other = 1 - core
    node_rows, cls = logits.shape
    stripe = nz * node_rows
    slots = tiles_hbm.shape[0]
    tile_rows, tile_cols = stripe // 128, ny * nx
    finish = []

    def device(yy, xx, kk):
        return (yy * nx + xx) * 2 + kk, z

    def send(src, dst, to, send_id, recv):
        pltpu.make_async_remote_copy(
            src_ref=src, dst_ref=dst, send_sem=send_sem.at[send_id], recv_sem=recv,
            device_id=to, device_id_type=MESH,
        ).start()

    def await_bytes(ref, sem):
        if 0 in ref.shape:
            return
        pltpu.make_async_copy(ref, ref, sem).wait()

    def sent(ref, send_id, some=1):
        if some:
            finish.append(lambda: await_bytes(ref, send_sem.at[send_id]))

    def load(src, dst, i):
        copy = pltpu.make_async_copy(src, dst, local_sem.at[i])
        copy.start()
        return copy

    feat_copy, deg_copy = load(feat_hbm, feat, 0), load(deg_hbm, deg, 1)
    slots_copy, count_copy = load(slots_hbm, slots_at, 2), load(counts_hbm, count_at, 3)

    barrier = pltpu.get_barrier_semaphore()

    def greet(to):
        pl.semaphore_signal(barrier, inc=1, device_id=to, device_id_type=MESH)

    for step in range(1, ny):
        greet(device(lax.rem(y + step, ny), x, core))
    for step in range(1, nx):
        greet(device(y, lax.rem(x + step, nx), core))
    greet(device(y, x, other))

    @pl.loop(1, nz)
    def _(step):
        greet((row, lax.rem(z + step, nz)))

    tiles_copy, cot_copy = load(tiles_hbm, tiles.at[pl.ds(0, slots)], 4), load(cot_hbm, cot, 5)
    w1_copy, w2_copy = load(w1_hbm, w1, 6), load(w2t_hbm, w2t, 7)
    feat_copy.wait()
    deg_copy.wait()

    per_line = 128 // node_rows
    line = lax.rsqrt(deg[pl.ds(z // per_line, 1), :].astype(F32))
    own_scale[...] = jnp.broadcast_to(line, (128, 128)).T
    own = own_scale[pl.ds(pl.multiple_of(lax.rem(z, per_line) * node_rows, node_rows), node_rows), :]
    own_wide = jnp.concatenate([own, own], axis=1)
    g1[y, x, core] = (own * feat[...].astype(F32)).astype(BF16)

    pl.semaphore_wait(barrier, (ny - 1) + (nx - 1) + 1 + (nz - 1))

    y_order = sorted(range(1, ny), key=lambda step: min(step, ny - step))

    pairs = ny // 2

    def gather_start(g, ysem, xsem, ids):
        mine = g.at[y, x, core]
        for step in y_order:
            send(mine, mine, device(lax.rem(y + step, ny), x, core), ids, ysem.at[y])
        for step in range(1, nx):
            to = device(y, lax.rem(x + step, nx), core)
            send(mine, mine, to, ids + 1, xsem.at[x, y // 2])
        sent(g.at[pl.ds(0, ny - 1), 0, 0], ids)
        sent(g.at[:, pl.ds(0, nx - 1), 0], ids + 1, nx - 1)
        sent(g.at[:, :, 0], ids + 2)

    def gather_rows(g, ysem, xsem, ssem, ids):
        for step in y_order:
            yy = lax.rem(y + step, ny)
            block = g.at[yy, x, core]
            await_bytes(block, ysem.at[yy])
            for side in range(1, nx):
                to = device(y, lax.rem(x + side, nx), core)
                send(block, block, to, ids + 1, xsem.at[x, yy // 2])
        for pair in range(pairs):
            blocks = g.at[pl.ds(pair * 2, 2), x, core]
            send(blocks, blocks, device(y, x, other), ids + 2, ssem.at[pair])

    def gather_columns(g, xsem, ssem, ids, steps):
        for step in steps:
            pair = lax.rem(y // 2 + step, pairs)
            for side in range(1, nx):
                xx = lax.rem(x + side, nx)
                blocks = g.at[pl.ds(pair * 2, 2), xx, core]
                await_bytes(blocks, xsem.at[xx, pair])
                send(blocks, blocks, device(y, x, other), ids + 2, ssem.at[pair])

    pair_order = sorted(range(pairs), key=lambda step: min(step, pairs - step))

    span = min(256, stripe)
    peers, parts = span // node_rows, stripe // span

    def gather_finish(g, ssem):
        for pair in range(pairs):
            await_bytes(g.at[pl.ds(pair * 2, 2), :, other], ssem.at[pair])

    def unpack(first_line, lines, k):
        @pl.loop(0, lines * nx)
        def _(i):
            line, xx = first_line + i // nx, lax.rem(i, nx)
            block = g2[line, xx, k]
            tail = block[node_rows:].astype(F32)
            tail = jnp.concatenate([tail, pltpu.roll(tail, 64, 1)], axis=0).astype(BF16)
            first = ((line * nx + xx) * 2 + k) * node_rows
            rows = pl.ds(pl.multiple_of(first, node_rows), node_rows)
            source[rows, :128] = block[:node_rows]
            source[rows, 128:] = tail

    reach = nz // 4

    def aggregate(source_of, pack, p, r, ids, sem, far_sem, between=None):
        half = p.shape[1] // 2

        def one(i):
            part = i
            if parts == 4:
                turn = (1 - i // 2) * (2 + i) + (i // 2) * (3 - i)
                part = lax.rem(z // peers + turn, parts)
            rows = adjacency[pl.ds(pl.multiple_of(part * span, span), span), :]
            value = dot(rows, source_of())
            for peer in range(peers):
                to = part * peers + peer
                p[to] = pack(value[peer * node_rows:(peer + 1) * node_rows])
                ahead = lax.rem(to - z + nz, nz)

                if reach > 1:
                    @pl.when(lax.rem(ahead, reach) != 0)
                    def _():
                        side = 1 - ahead // (nz // 2)
                        away = side * ahead + (1 - side) * (nz - ahead)
                        far = (away - 1) // reach
                        hop = away - reach * far
                        slot = far * (2 * reach + side * (reach - 1)) + (1 - far) * side * reach + hop - 1
                        target = lax.rem(z + (2 * side - 1) * hop + nz, nz)
                        send(p.at[to], r.at[slot], (row, target), ids, one_sem.at[sem + far * (far_sem - sem)])

                @pl.when(ahead == nz // 2)
                def _():
                    for side in range(2):
                        rows = pl.ds(side * half, half)
                        target = lax.rem(z + (2 * side - 1) * reach + nz, nz)
                        send(p.at[to, rows], r.at[4 * reach - 2, rows], (row, target), ids, one_sem.at[far_sem])

        middle = parts // 2 if between else 0
        if between:
            pl.loop(0, middle)(one)
            between()
        pl.loop(middle, parts)(one)
        r[4 * reach - 1] = p[z]
        sent(r.at[pl.ds(0, nz - 1)], ids)

    def relay(p, r, q, ids, sem, far_sem):
        half = p.shape[1] // 2
        await_bytes(r.at[pl.ds(2 * reach, 2 * reach - 1)], one_sem.at[far_sem])
        opposite = r[4 * reach - 2].astype(F32)
        nothing = jnp.zeros((half, 128), F32)
        for side in range(2):
            to = lax.rem(z + (2 * side - 1) * reach + nz, nz)
            first = 2 * reach + side * (reach - 1)
            part = (
                jnp.concatenate([nothing, opposite[half:]], axis=0) if side
                else jnp.concatenate([opposite[:half], nothing], axis=0)
            )
            value = total([part, p[to].astype(F32)] + [r[first + i].astype(F32) for i in range(reach - 1)])
            q[side] = value.astype(BF16)
            send(q.at[side], r.at[side * reach + reach - 1], (row, to), ids, one_sem.at[sem])

    def aggregate_sum(r, sem):
        await_bytes(r.at[pl.ds(0, 2 * reach)], one_sem.at[sem])
        return total(r[i].astype(F32) for i in list(range(2 * reach)) + [4 * reach - 1])

    short = node_rows // 2
    low_lanes = lax.broadcasted_iota(jnp.int32, (short, 128), 1) < 64

    def pack_classes(value):
        first, second = value[:short, 128:], pltpu.roll(value[short:, 128:], 64, 1)
        tail = jnp.where(low_lanes, first, second)
        return jnp.concatenate([value[:, :128], tail], axis=0).astype(BF16)

    def finish_all():
        for wait in finish:
            wait()


    gather_start(g1, g1y, g1x, 0)

    slots_copy.wait()
    count_copy.wait()
    cells = lax.broadcasted_iota(jnp.int32, (8, 128), 0) * 128 + lax.broadcasted_iota(jnp.int32, (8, 128), 1)
    count = count_at[0]
    held = jnp.full((8, 128), slots, jnp.int32)
    for t in range(slots):
        held = jnp.where((cells == slots_at[0, t]) & (t < count), t, held)
    table_v[...] = held
    table_copy = load(table_v, table, 8)
    tiles_copy.wait()
    tiles[slots] = jnp.zeros((128, 128), BF16)
    table_copy.wait()

    @pl.loop(0, tile_cols)
    def _(c):
        for r in range(tile_rows):
            adjacency[r * 128:(r + 1) * 128, pl.ds(pl.multiple_of(c * 128, 128), 128)] = tiles[
                table[r * tile_cols // 128, lax.rem(r * tile_cols, 128) + c]
            ]

    gather_rows(g1, g1y, g1x, g1s, 0)

    cot_copy.wait()
    scot[cls // 16 * 16:, :] = jnp.zeros((2 * HALF - cls // 16 * 16, stripe), BF16)
    for r in range(tile_rows):
        by = lax.rsqrt(deg[r:r + 1, :].astype(F32))
        scot[:cls, r * 128:(r + 1) * 128] = (
            cot[:, r * 128:(r + 1) * 128].astype(F32) * by
        ).astype(BF16)
    w1_copy.wait()
    w2_copy.wait()
    w2p[cls // 16 * 16:, :] = jnp.zeros((w2p.shape[0] - cls // 16 * 16, w2p.shape[1]), BF16)
    w2p[:cls, :] = w2t[...]

    @pl.loop(0, ny)
    def _(part):
        columns = pl.ds(pl.multiple_of(part * nx * 128, nx * 128), nx * 128)
        value = dot(scot[...], adjacency[:, columns]).astype(BF16)
        for xx in range(nx):
            terms[part, xx] = value[:, xx * 128:(xx + 1) * 128].reshape(2, HALF, 128)
        send(terms.at[part, :, other], sib.at[part], device(y, x, other), 6, one_sem.at[0])

    sent(sib, 6)

    gather_columns(g1, g1x, g1s, 0, pair_order)

    await_bytes(sib, one_sem.at[0])

    @pl.loop(0, ny)
    def _(part):
        for xx in range(nx):
            tsum[xx, part] = (
                terms[part, xx, core].astype(F32) + sib[part, xx].astype(F32)
            ).astype(BF16)

    for side in range(1, nx):
        xx = lax.rem(x + side, nx)
        send(tsum.at[xx], tx.at[x], device(y, xx, core), 8, one_sem.at[2])
    sent(tx.at[pl.ds(0, nx - 1)], 8, nx - 1)
    tx[x] = tsum[x]

    gather_finish(g1, g1s)
    nodes = tile_cols * 128
    aggregate(lambda: g1[...].reshape(nodes, 128), lambda v: v.astype(BF16), p1, r1, 7, 1, 13)
    relay(p1, r1, q1, 7, 1, 13)

    await_bytes(tx.at[pl.ds(0, nx - 1)], one_sem.at[2])

    @pl.loop(0, ny)
    def _(part):
        tsum[x, part] = total(tx[i, part].astype(F32) for i in range(nx)).astype(BF16)

    for step in y_order:
        yy = lax.rem(y + step, ny)
        send(tsum.at[x, yy], ty.at[y], device(yy, x, core), 9, one_sem.at[3])
    sent(ty.at[pl.ds(0, ny - 1)], 9)
    ty[y] = tsum[x, y]

    first_agg = (own * aggregate_sum(r1, 1)).astype(BF16)
    first_pre = dot(first_agg, w1[...])
    bend = jnp.tanh(CURVE * (first_pre + CUBIC * first_pre * first_pre * first_pre))
    hidden = (own_wide * (0.5 * first_pre * (1.0 + bend))).astype(BF16)
    g2[y, x, core] = pack_classes(dot(hidden, w2p[...], ((1,), (1,))))
    gather_start(g2, g2y, g2x, 3)

    slope = 0.5 * (1.0 + bend) + 0.5 * first_pre * (1.0 - bend * bend) * (
        CURVE * (1.0 + 3.0 * CUBIC * first_pre * first_pre)
    )

    await_bytes(ty.at[pl.ds(0, ny - 1)], one_sem.at[3])
    narrow_t[core] = total(ty[i].astype(F32) for i in range(ny))
    mine = narrow_t.at[core]
    send(mine, mine, device(y, x, other), 18, one_sem.at[12])
    sent(mine, 18)

    n_first, hid = out_first.shape
    chunk = gz.shape[1]
    await_bytes(narrow_t.at[0], one_sem.at[12])
    lane_core = lax.broadcasted_iota(jnp.int32, (2 * HALF, 128), 1) // node_rows
    narrow = jnp.where(lane_core == core, narrow_t[...].reshape(2 * HALF, 128), 0.0)
    high, low = split(narrow)
    w2_rows = w2p[:2 * HALF, :]
    back_all[...] = dot(high, w2_rows, ((0,), (0,))) + dot(low, w2_rows, ((0,), (0,)))
    back = back_all[pl.ds(pl.multiple_of(core * node_rows, node_rows), node_rows), :]
    grad_pre = (own_wide * back * slope).astype(BF16)
    first_rows = dot(first_agg, grad_pre, ((0,), (0,)))
    hidden_twice = jnp.concatenate([hidden, hidden], axis=0)
    second_rows = dot(high, hidden_twice) + dot(low, hidden_twice)
    spare = 2 * nx * ny * chunk - n_first - 2 * HALF
    grad[...] = jnp.concatenate(
        [first_rows, second_rows, jnp.zeros((spare, hid), F32)], axis=0
    ).reshape(grad.shape)
    send(grad.at[other], gsib, device(y, x, other), 10, one_sem.at[4])
    sent(gsib, 10)

    gather_rows(g2, g2y, g2x, g2s, 3)

    await_bytes(gsib, one_sem.at[4])
    gys[...] = (gsib[...] + grad[core]).astype(BF16)
    for step in y_order:
        yy = lax.rem(y + step, ny)
        send(gys.at[yy], gy.at[y], device(yy, x, core), 11, one_sem.at[5])
    sent(gy.at[pl.ds(0, ny - 1)], 11)
    gy[y] = gys[y]

    def second_columns(steps):
        for step in steps:
            gather_columns(g2, g2x, g2s, 3, [step])
            unpack(lax.rem(y // 2 + step, pairs) * 2, 2, core)

    second_columns(pair_order[:2])

    await_bytes(gy.at[pl.ds(0, ny - 1)], one_sem.at[5])
    gxs[...] = total(gy[i].astype(F32) for i in range(ny)).reshape(nx, chunk, hid)
    for side in range(1, nx):
        xx = lax.rem(x + side, nx)
        send(gxs.at[xx], gx.at[x], device(y, xx, core), 13, one_sem.at[7])
    sent(gx.at[pl.ds(0, nx - 1)], 13, nx - 1)
    gx[x] = gxs[x]

    second_columns(pair_order[2:])

    await_bytes(gx.at[pl.ds(0, nx - 1)], one_sem.at[7])
    group, member = z // 4, lax.rem(z, 4)
    gz[member] = total(gx[i] for i in range(nx))
    for step in range(1, 4):
        to = group * 4 + lax.rem(member + step, 4)
        send(gz.at[member], gz.at[member], (row, to), 14, one_sem.at[8])
    sent(gz.at[pl.ds(0, 3)], 14)

    gather_finish(g2, g2s)
    unpack(0, ny, other)

    groups = nz // 4
    await_bytes(gz.at[pl.ds(0, 3)], one_sem.at[8])
    gw[group] = total(gz[i] for i in range(4))
    for step in range(1, groups):
        to = lax.rem(group + step, groups) * 4 + member
        send(gw.at[group], gw.at[group], (row, to), 19, one_sem.at[15])
    sent(gw.at[pl.ds(0, groups - 1)], 19, groups - 1)

    def spread_y():
        await_bytes(gw.at[pl.ds(0, groups - 1)], one_sem.at[15])
        gfull[core, y, x] = total(gw[i] for i in range(groups))
        mine_y = gfull.at[core, y, x]
        for step in y_order:
            send(mine_y, mine_y, device(lax.rem(y + step, ny), x, core), 15, one_sem.at[9])
        sent(gfull.at[0, pl.ds(0, ny - 1), 0], 15)

    aggregate(lambda: source[...], pack_classes, p2, r2, 12, 6, 14, spread_y)
    relay(p2, r2, q2, 12, 6, 14)

    await_bytes(gfull.at[0, pl.ds(0, ny - 1), 0], one_sem.at[9])
    mine_x = gfull.at[core, :, x]
    for side in range(1, nx):
        send(mine_x, mine_x, device(y, lax.rem(x + side, nx), core), 16, one_sem.at[10])
    sent(gfull.at[0, :, pl.ds(0, nx - 1)], 16, nx - 1)
    await_bytes(gfull.at[0, :, pl.ds(0, nx - 1)], one_sem.at[10])
    send(gfull.at[core], gfull.at[core], device(y, x, other), 17, one_sem.at[11])
    sent(gfull.at[0], 17)

    packed = aggregate_sum(r2, 6)
    tail = packed[node_rows:]
    tail = jnp.concatenate([tail, pltpu.roll(tail, 64, 1)], axis=0)
    logits[:, :128] = (own * packed[:node_rows]).astype(BF16)
    logits[:, 128:] = (own * tail)[:, :cls - 128].astype(BF16)

    await_bytes(gfull.at[0], one_sem.at[11])
    whole = gfull[...].reshape(2 * nx * ny * chunk, hid)
    out_first[...] = whole[:n_first]
    out_second[...] = whole[n_first:n_first + cls]

    finish_all()


def hand_out(a, b, c, a_out, b_out, c_out):
    a_out[...] = a[...]
    b_out[...] = b[...]
    c_out[...] = c[...]


def shards(dims, features, degrees, tiles, tile_slots, tile_counts, w_first, w_second, cotangent):
    nx, ny, nz = dims
    node_rows, f_in = features.shape
    slots = tiles.shape[1]
    hid, cls = w_second.shape
    stripe = nz * node_rows
    tile_rows, tile_cols = stripe // 128, ny * nx
    chunk = 512 // (2 * nx * ny)
    vmem = pl.BlockSpec(memory_space=pltpu.VMEM)
    far = pl.BlockSpec(memory_space=pltpu.HBM)
    scratch = lambda *shape, dtype=BF16: pltpu.VMEM(shape, dtype)
    sems = lambda *shape: pltpu.SemaphoreType.DMA(shape)
    results = pl.pallas_call(
        functools.partial(kernel, dims),
        out_shape=(
            jax.ShapeDtypeStruct((node_rows, cls), BF16),
            jax.ShapeDtypeStruct((f_in, hid), F32),
            jax.ShapeDtypeStruct((cls, hid), F32),
        ),
        in_specs=[far] * 8,
        out_specs=(vmem, vmem, vmem),
        scratch_shapes=[
            scratch(node_rows, f_in),
            scratch(tile_rows, 128, dtype=jnp.int32),
            scratch(slots + 1, 128, 128),
            pltpu.SMEM((1, slots), jnp.int32),
            pltpu.SMEM((1,), jnp.int32),
            scratch(f_in, hid),
            scratch(cls, hid),
            scratch(cls, stripe),
            scratch(8, 128, dtype=jnp.int32),
            pltpu.SMEM((8, 128), jnp.int32),
            scratch(stripe, tile_cols * 128),
            scratch(2 * HALF, stripe),
            scratch(256, hid),
            scratch(128, 128, dtype=F32),
            scratch(ny, nx, 2, node_rows, f_in),
            scratch(ny, nx, 2, HALF, 128),
            scratch(tile_cols * 128, 256),
            scratch(nz, node_rows, f_in),
            scratch(nz, node_rows, f_in),
            scratch(2, node_rows, f_in),
            scratch(nz, HALF, 128),
            scratch(nz, HALF, 128),
            scratch(2, HALF, 128),
            scratch(ny, nx, 2, HALF, 128),
            scratch(ny, nx, HALF, 128),
            scratch(nx, ny, HALF, 128),
            scratch(nx, ny, HALF, 128),
            scratch(ny, HALF, 128),
            scratch(2, HALF, 128, dtype=F32),
            scratch(128, hid, dtype=F32),
            scratch(2, ny, nx * chunk, hid, dtype=F32),
            scratch(ny, nx * chunk, hid, dtype=F32),
            scratch(ny, nx * chunk, hid),
            scratch(ny, nx * chunk, hid),
            scratch(nx, chunk, hid, dtype=F32),
            scratch(nx, chunk, hid, dtype=F32),
            scratch(4, chunk, hid, dtype=F32),
            scratch(nz // 4, chunk, hid, dtype=F32),
            scratch(2, ny, nx, chunk, hid, dtype=F32),
            sems(9),
            sems(20),
            sems(ny), sems(nx, ny // 2), sems(ny // 2),
            sems(ny), sems(nx, ny // 2), sems(ny // 2),
            sems(16),
        ],
        compiler_params=pltpu.CompilerParams(
            collective_id=0, has_side_effects=True, vmem_limit_bytes=LIMIT
        ),
    )(
        features, degrees.reshape(tile_rows, 128), tiles[0], tile_slots, tile_counts, w_first,
        w_second.T, cotangent.T
    )
    logits, grad_first, grad_second = pl.pallas_call(
        hand_out,
        out_shape=tuple(jax.ShapeDtypeStruct(a.shape, a.dtype) for a in results),
        in_specs=[vmem] * 3,
        out_specs=(vmem,) * 3,
        compiler_params=pltpu.CompilerParams(vmem_limit_bytes=LIMIT),
    )(*results)
    return logits, grad_first, grad_second.T


def solution(mesh):
    ny = 8 if mesh.shape["row"] == 64 else 2
    dims = (mesh.shape["row"] // (2 * ny), ny, mesh.shape["col"])
    placed = (
        P(("row", "col"), None),
        P("row"),
        P(("row", "col"), None, None, None),
        P(("row", "col"), None),
        P(("row", "col")),
        P(),
        P(),
        P("row", None),
    )
    return jax.shard_map(
        functools.partial(shards, dims),
        mesh=mesh,
        in_specs=placed,
        out_specs=(P(("row", "col"), None), P(), P()),
        check_vma=False,
    )
```
